32 devices in a mesh: dp: 8 (over y, x, core), tensor: 4 (over z).
Axes of the slice: x: 2, y: 2, z: 4, core: 2. Of those that a mesh axis runs over, the one named last changes fastest.
Arguments:
- hidden: bfloat16 [1024, 8192], P('dp', 'tensor')
- rotation: float32 [8192, 8192], P('dp', 'tensor'), may hold values from -0.0625 to 0.0625
- channel_scale: float32 [8192], P('tensor')
- lengths: int32 [16], P('dp'), may hold values from 16 to 64, as said below
Outputs:
- direction: float32 [8192, 8192], P('dp', 'tensor')
- loss: float32 [], replicated
The draws below stay inside these ranges and needn't reach their ends.
Inputs may be any that keep to these rules, and one draw needn't show every extreme that they name: `lengths`: each sequence's valid length; some sequence is full in every draw.
All inputs are finite; a program needn't handle non-finite values.
Results may differ from the reference program's by a relative error of at most 0.00075.
The reference program's roundings to bfloat16 on the way (of `narrow_rotation` and `error_slope`) count: a program that leaves them out, or rounds other values in their place, can miss the bound.
Values may be sent and summed in bfloat16 or wider, within the bound.
A program may use at most 128 MiB of HBM per device.

```python
import math
import jax
import jax.numpy as jnp
from jax import lax

D = 8192
SEQ = 64
SEQS = 16
TOKENS = 1024


def draw_hidden(key, part):
    first, second = jax.random.split(key, 2)
    ramp = jnp.arange(D, dtype=jnp.float32) / (D - 1)
    column = jnp.exp(jax.random.uniform(second, (D,), jnp.float32, 0.0, math.log(10.0))) * 3.0 ** ramp
    base = jax.random.normal(first, (TOKENS, D), jnp.float32)
    return (base * column[None, :] / 3.0).astype(jnp.bfloat16)


def draw_channel_scale(key, part):
    ramp = jnp.arange(D, dtype=jnp.float32) / (D - 1)
    spread = jnp.exp(jax.random.uniform(key, (D,), jnp.float32, math.log(0.5), math.log(2.0)))
    return spread * 3.0 ** ramp / 2.0


def draw_lengths(key, part):
    first, second = jax.random.split(key)
    values = jax.random.randint(first, (SEQS,), SEQ // 4, SEQ + 1, dtype=jnp.int32)
    chosen = jax.random.randint(second, (), 0, SEQS, dtype=jnp.int32)
    return jnp.where(jnp.arange(SEQS, dtype=jnp.int32) == chosen, SEQ, values).astype(jnp.int32)


def level_of(key, shape, cuts, low, largest):
    def one(dim, parts):
        draws = jax.random.uniform(jax.random.fold_in(jax.random.fold_in(key, 6), dim), (parts,), jnp.float32, low / len(cuts), largest / len(cuts))
        return jnp.repeat(jnp.exp(draws), shape[dim] // parts).reshape((-1,) + (1,) * (len(shape) - dim - 1))

    gain = one(*cuts[0])
    for cut in cuts[1:]:
        gain = gain * one(*cut)
    return gain


def centred(own_key, shape, scale, most, cuts=(), kind=jnp.bfloat16):
    values = jax.random.normal(own_key, shape, jnp.float32) * scale
    if len(cuts) > 0:
        values = level_of(own_key, shape, cuts, -0.22, 0.18) * values
    return jnp.clip(values, min=-most, max=most).astype(kind)


def setup_inputs(seed: int = 0) -> dict:
    seeds = jax.random.split(jax.random.key(seed), 5)
    return {
        "hidden": draw_hidden(jax.random.fold_in(seeds[4], 71), 0),
        "rotation": centred(seeds[1], (D, D), D ** -0.5, 0.0625, ((0, 8), (1, 4)), jnp.float32),
        "channel_scale": draw_channel_scale(jax.random.fold_in(seeds[4], 71), 0),
        "lengths": draw_lengths(jax.random.fold_in(seeds[4], 71), 0),
    }


def reference(hidden, rotation, channel_scale, lengths):
    narrow_rotation = rotation.astype(jnp.bfloat16)
    rotated = jnp.dot(hidden, narrow_rotation, preferred_element_type=jnp.float32)
    scaled = rotated * channel_scale[None, :]
    step_size = 4.0 * jnp.sqrt(lax.optimization_barrier(jnp.mean(scaled * scaled, axis=1)) + 1e-06)[:, None]
    token_index = jnp.arange(TOKENS, dtype=jnp.int32)
    position = token_index % SEQ
    sequence_index = token_index // SEQ
    live_mask = jnp.where(position < lengths[sequence_index], 1.0, 0.0).astype(jnp.float32)[:, None]
    angles = math.pi * scaled / step_size
    error_sum = jnp.sum(live_mask * jnp.sin(angles) ** 2)
    count = jnp.sum(lengths).astype(jnp.float32)
    loss = error_sum / (D * count)
    error_slope = (live_mask * (math.pi / step_size) * jnp.sin(2.0 * angles) * channel_scale[None, :]).astype(jnp.bfloat16)
    gradient = jnp.dot(hidden.T, error_slope, preferred_element_type=jnp.float32)
    direction = gradient / jnp.sqrt(jnp.mean(gradient * gradient) + 1e-06)
    return (direction, loss)
```

```python
import math

import jax
import jax.numpy as jnp
from jax import lax
from jax.sharding import PartitionSpec as P

D = 8192
SEQ = 64


def local(hidden, rotation, channel_scale, lengths):
    narrow_rotation = rotation.astype(jnp.bfloat16)
    features = lax.all_gather(hidden, "tensor", axis=1, tiled=True)
    column_blocks = lax.all_to_all(features, "dp", split_axis=1, concat_axis=0, tiled=True)
    partial = jnp.dot(column_blocks, narrow_rotation, preferred_element_type=jnp.float32)
    rotated = lax.psum_scatter(partial, "dp", scatter_dimension=0, tiled=True)
    scaled = rotated * channel_scale[None, :]
    token_square = lax.psum(jnp.sum(scaled * scaled, axis=1), "tensor")
    step_size = 4.0 * jnp.sqrt(token_square / D + 1e-06)[:, None]
    token_index = jnp.arange(hidden.shape[0], dtype=jnp.int32)
    position = token_index % SEQ
    sequence_index = token_index // SEQ
    sequence_count = lengths.shape[0]
    owners = sequence_index[:, None] == jnp.arange(sequence_count, dtype=jnp.int32)[None, :]
    inside = position[:, None] < lengths[None, :]
    live_mask = jnp.sum(jnp.where(owners & inside, 1.0, 0.0), axis=1).astype(jnp.float32)[:, None]
    angles = math.pi * scaled / step_size
    error_local = jnp.sum(live_mask * jnp.sin(angles) ** 2)
    count_local = jnp.sum(lengths).astype(jnp.float32) / lax.axis_size("tensor")
    error_slope = (
        live_mask * (math.pi / step_size) * jnp.sin(2.0 * angles) * channel_scale[None, :]
    ).astype(jnp.bfloat16)
    gradient = lax.dot_general(
        column_blocks,
        lax.all_gather(error_slope, "dp", axis=0, tiled=True),
        (((0,), (0,)), ((), ())),
        preferred_element_type=jnp.float32,
    )
    error_sum, count = lax.psum((error_local, count_local), ("dp", "tensor"))
    grad_square = lax.psum(jnp.sum(gradient * gradient), ("dp", "tensor"))
    direction = gradient / jnp.sqrt(grad_square / (D * D) + 1e-06)
    loss = error_sum / (D * count)
    return (direction, loss)


def solution(mesh):
    return jax.shard_map(
        local,
        mesh=mesh,
        in_specs=(P("dp", "tensor"), P("dp", "tensor"), P("tensor"), P("dp")),
        out_specs=(P("dp", "tensor"), P()),
        check_vma=False,
    )
```

```python
import functools
import math

import jax
import jax.numpy as jnp
from jax import lax
from jax.experimental import pallas as pl
from jax.experimental.pallas import tpu as pltpu
from jax.sharding import PartitionSpec as P

D = 8192
SEQ = 64
MESH = pl.DeviceIdType.MESH


def greet(axes):
    barrier = pltpu.get_barrier_semaphore()
    total = 0
    for axis, n in axes:
        me = lax.axis_index(axis)
        for off in range(1, n):
            pl.semaphore_signal(barrier, inc=1, device_id={axis: lax.rem(me + off, n)}, device_id_type=MESH)
        total += n - 1
    pl.semaphore_wait(barrier, total)


def all_sum(axis, n, slots, send, recv, value):
    me = lax.axis_index(axis)
    slots[me] = value
    copies = []
    for off in range(1, n):
        copy = pltpu.make_async_remote_copy(
            src_ref=slots.at[me],
            dst_ref=slots.at[me],
            send_sem=send.at[off],
            recv_sem=recv.at[off],
            device_id={axis: lax.rem(me + off, n)},
            device_id_type=MESH,
        )
        copy.start()
        copies.append(copy)
    for copy in copies:
        copy.wait()
    return jnp.sum(slots[...], axis=0)


def token_kernel(nt, x_ref, o_ref, slots, send, recv):
    greet([("tensor", nt)])
    o_ref[...] = all_sum("tensor", nt, slots, send, recv, x_ref[...])


def token_sum(nt, x):
    return pl.pallas_call(
        functools.partial(token_kernel, nt),
        out_shape=jax.ShapeDtypeStruct(x.shape, jnp.float32),
        in_specs=[pl.BlockSpec(memory_space=pltpu.VMEM)],
        out_specs=pl.BlockSpec(memory_space=pltpu.VMEM),
        scratch_shapes=[
            pltpu.VMEM((nt,) + x.shape, jnp.float32),
            pltpu.SemaphoreType.DMA((nt,)),
            pltpu.SemaphoreType.DMA((nt,)),
        ],
        compiler_params=pltpu.CompilerParams(collective_id=0, has_side_effects=True),
    )(x)


def gradient_kernel(nd, nt, tile, h_ref, s_ref, extra_ref, g_ref, o_ref, buf, out_sem, tslots, dslots, ts, tr, ds, dr):
    greet([("dp", nd), ("tensor", nt)])
    rows, columns = g_ref.shape
    steps = columns // tile
    square = jnp.zeros((8, tile), jnp.float32)
    copies = []
    for step in range(steps):
        slot = step % 2
        if step >= 2:
            copies[step - 2].wait()
        block = jnp.dot(h_ref[...], s_ref[:, step * tile:(step + 1) * tile], preferred_element_type=jnp.float32)
        buf[slot] = block
        square = square + jnp.sum((block * block).reshape(rows // 8, 8, tile), axis=0)
        copy = pltpu.make_async_copy(buf.at[slot], g_ref.at[:, pl.ds(step * tile, tile)], out_sem.at[slot])
        copy.start()
        copies.append(copy)
    row = lax.broadcasted_iota(jnp.int32, (8, 128), 0)
    value = extra_ref[...] + jnp.where(row == 0, jnp.sum(square), 0.0)
    value = all_sum("tensor", nt, tslots, ts, tr, value)
    o_ref[...] = all_sum("dp", nd, dslots, ds, dr, value)
    for copy in copies[-2:]:
        copy.wait()


def gradient_call(nd, nt, h, s, extra):
    rows, columns = h.shape[0], s.shape[1]
    tile = 256
    vmem = pl.BlockSpec(memory_space=pltpu.VMEM)
    dma = pltpu.SemaphoreType.DMA
    return pl.pallas_call(
        functools.partial(gradient_kernel, nd, nt, tile),
        out_shape=(
            jax.ShapeDtypeStruct((rows, columns), jnp.float32),
            jax.ShapeDtypeStruct((8, 128), jnp.float32),
        ),
        in_specs=[vmem, vmem, vmem],
        out_specs=(pl.BlockSpec(memory_space=pl.ANY), vmem),
        scratch_shapes=[
            pltpu.VMEM((2, rows, tile), jnp.float32),
            dma((2,)),
            pltpu.VMEM((nt, 8, 128), jnp.float32),
            pltpu.VMEM((nd, 8, 128), jnp.float32),
            dma((nt,)),
            dma((nt,)),
            dma((nd,)),
            dma((nd,)),
        ],
        compiler_params=pltpu.CompilerParams(
            collective_id=1, has_side_effects=True, vmem_limit_bytes=40 * 1024 * 1024
        ),
    )(h, s, extra)


def sin_cos_pi(turns):
    v = turns - jnp.round(turns)
    x = math.pi * v
    z = x * x
    s = x * (1.0 + z * (-1 / 6 + z * (1 / 120 + z * (-1 / 5040 + z * (1 / 362880 - z * (1 / 39916800))))))
    c = 1.0 + z * (-0.5 + z * (1 / 24 + z * (-1 / 720 + z * (1 / 40320 + z * (-1 / 3628800 + z * (1 / 479001600))))))
    return s, c


def local(hidden, rotation, channel_scale, lengths):
    nd, nt = lax.axis_size("dp"), lax.axis_size("tensor")
    tokens = hidden.shape[0]
    narrow_rotation = rotation.astype(jnp.bfloat16)
    features = lax.all_gather(hidden, "tensor", axis=1, tiled=True)
    column_blocks = lax.all_to_all(features, "dp", split_axis=1, concat_axis=0, tiled=True)
    partial = jnp.dot(column_blocks, narrow_rotation, preferred_element_type=jnp.float32)
    rotated = lax.psum_scatter(partial, "dp", scatter_dimension=0, tiled=True)
    scaled = rotated * channel_scale[None, :]
    own_square = jnp.sum(scaled * scaled, axis=1)
    token_square = token_sum(nt, jnp.broadcast_to(own_square[None, :], (8, tokens)))[0]
    step_size = 4.0 * jnp.sqrt(token_square / D + 1e-06)[:, None]
    token_index = jnp.arange(tokens, dtype=jnp.int32)
    position = token_index % SEQ
    sequence_index = token_index // SEQ
    sequence_count = lengths.shape[0]
    owners = sequence_index[:, None] == jnp.arange(sequence_count, dtype=jnp.int32)[None, :]
    inside = position[:, None] < lengths[None, :]
    live_mask = jnp.sum(jnp.where(owners & inside, 1.0, 0.0), axis=1).astype(jnp.float32)[:, None]
    sine, cosine = sin_cos_pi(scaled / step_size)
    error_local = jnp.sum(live_mask * sine * sine)
    count_local = jnp.sum(lengths).astype(jnp.float32) / nt
    error_slope = (
        live_mask * (math.pi / step_size) * (2.0 * sine * cosine) * channel_scale[None, :]
    ).astype(jnp.bfloat16)
    slopes = lax.all_gather(error_slope, "dp", axis=0, tiled=True)
    row = lax.broadcasted_iota(jnp.int32, (8, 128), 0)
    extra = jnp.where(row == 1, error_local, jnp.where(row == 2, count_local, 0.0))
    gradient, totals = gradient_call(nd, nt, column_blocks.T, slopes, extra)
    direction = gradient * (1.0 / jnp.sqrt(totals[0, 0] / (D * D) + 1e-06))
    loss = totals[1, 0] / (D * totals[2, 0])
    return (direction, loss)


def solution(mesh):
    return jax.shard_map(
        local,
        mesh=mesh,
        in_specs=(P("dp", "tensor"), P("dp", "tensor"), P("tensor"), P("dp")),
        out_specs=(P("dp", "tensor"), P()),
        check_vma=False,
    )
```

```python
import functools
import math

import jax
import jax.numpy as jnp
from jax import lax
from jax.experimental import pallas as pl
from jax.experimental.pallas import tpu as pltpu
from jax.sharding import PartitionSpec as P

D = 8192
SEQ = 64
MESH = pl.DeviceIdType.MESH


def greet(axes):
    barrier = pltpu.get_barrier_semaphore()
    total = 0
    for axis, n in axes:
        me = lax.axis_index(axis)
        for off in range(1, n):
            pl.semaphore_signal(barrier, inc=1, device_id={axis: lax.rem(me + off, n)}, device_id_type=MESH)
        total += n - 1
    pl.semaphore_wait(barrier, total)


def all_sum(axis, n, slots, send, recv, value):
    me = lax.axis_index(axis)
    slots[me] = value
    copies = []
    for off in range(1, n):
        copy = pltpu.make_async_remote_copy(
            src_ref=slots.at[me],
            dst_ref=slots.at[me],
            send_sem=send.at[off],
            recv_sem=recv.at[off],
            device_id={axis: lax.rem(me + off, n)},
            device_id_type=MESH,
        )
        copy.start()
        copies.append(copy)
    for copy in copies:
        copy.wait()
    return jnp.sum(slots[...], axis=0)


def token_kernel(nt, x_ref, o_ref, slots, send, recv):
    greet([("tensor", nt)])
    o_ref[...] = all_sum("tensor", nt, slots, send, recv, x_ref[...])


def token_sum(nt, x):
    return pl.pallas_call(
        functools.partial(token_kernel, nt),
        out_shape=jax.ShapeDtypeStruct(x.shape, jnp.float32),
        in_specs=[pl.BlockSpec(memory_space=pltpu.VMEM)],
        out_specs=pl.BlockSpec(memory_space=pltpu.VMEM),
        scratch_shapes=[
            pltpu.VMEM((nt,) + x.shape, jnp.float32),
            pltpu.SemaphoreType.DMA((nt,)),
            pltpu.SemaphoreType.DMA((nt,)),
        ],
        compiler_params=pltpu.CompilerParams(collective_id=0, has_side_effects=True),
    )(x)


def gradient_kernel(nd, nt, tile, h_ref, s_ref, extra_ref, g_ref, o_ref, buf, out_sem, tslots, dslots, ts, tr, ds, dr):
    greet([("dp", nd), ("tensor", nt)])
    rows, columns = g_ref.shape
    steps = columns // tile
    square = jnp.zeros((8, tile), jnp.float32)
    copies = []
    for step in range(steps):
        slot = step % 2
        if step >= 2:
            copies[step - 2].wait()
        block = jnp.dot(h_ref[...], s_ref[:, step * tile:(step + 1) * tile], preferred_element_type=jnp.float32)
        buf[slot] = block
        square = square + jnp.sum((block * block).reshape(rows // 8, 8, tile), axis=0)
        copy = pltpu.make_async_copy(buf.at[slot], g_ref.at[:, pl.ds(step * tile, tile)], out_sem.at[slot])
        copy.start()
        copies.append(copy)
    row = lax.broadcasted_iota(jnp.int32, (8, 128), 0)
    value = extra_ref[...] + jnp.where(row == 0, jnp.sum(square), 0.0)
    value = all_sum("tensor", nt, tslots, ts, tr, value)
    o_ref[...] = all_sum("dp", nd, dslots, ds, dr, value)
    for copy in copies[-2:]:
        copy.wait()


def gradient_call(nd, nt, h, s, extra):
    rows, columns = h.shape[0], s.shape[1]
    tile = 256
    vmem = pl.BlockSpec(memory_space=pltpu.VMEM)
    dma = pltpu.SemaphoreType.DMA
    return pl.pallas_call(
        functools.partial(gradient_kernel, nd, nt, tile),
        out_shape=(
            jax.ShapeDtypeStruct((rows, columns), jnp.float32),
            jax.ShapeDtypeStruct((8, 128), jnp.float32),
        ),
        in_specs=[vmem, vmem, vmem],
        out_specs=(pl.BlockSpec(memory_space=pl.ANY), vmem),
        scratch_shapes=[
            pltpu.VMEM((2, rows, tile), jnp.float32),
            dma((2,)),
            pltpu.VMEM((nt, 8, 128), jnp.float32),
            pltpu.VMEM((nd, 8, 128), jnp.float32),
            dma((nt,)),
            dma((nt,)),
            dma((nd,)),
            dma((nd,)),
        ],
        compiler_params=pltpu.CompilerParams(
            collective_id=1, has_side_effects=True, vmem_limit_bytes=40 * 1024 * 1024
        ),
    )(h, s, extra)


def forward_kernel(nd, nt, hid_ref, w_ref, h_ref, r_ref, feats, part, mate_in, peer_in,
                   right_s, right_r, left_s, left_r, sc_s, sc_r, own_sem, mate_s, mate_r, peer_s, peer_r):
    greet([("dp", nd), ("tensor", nt)])
    i, j = lax.axis_index("dp"), lax.axis_index("tensor")
    t, width = hid_ref.shape
    depth = w_ref.shape[0]
    per = width // depth

    def rows(k):
        return h_ref.at[pl.ds(pl.multiple_of(k * t, t), t), :]

    def remote(src, dst, send, recv, target):
        return pltpu.make_async_remote_copy(
            src_ref=src, dst_ref=dst, send_sem=send, recv_sem=recv, device_id=target, device_id_type=MESH
        )

    def along(block, send, recv, to):
        return remote(feats.at[block], feats.at[block], send, recv, {"tensor": to})

    def spread(block):
        for h in range(per):
            dest = block * per + h
            piece = feats.at[block, :, pl.ds(h * depth, depth)]

            @pl.when(dest != i)
            def _():
                remote(piece, rows(i), sc_s.at[dest], sc_r.at[i], {"dp": dest}).start()

            @pl.when(dest == i)
            def _():
                pltpu.make_async_copy(piece, rows(i), own_sem.at[0]).start()

    feats[j] = hid_ref[...]
    for step in range(nt):
        if step < nt - 1:
            @pl.when((j - step >= 0) & (j < nt - 1))
            def _():
                along(lax.max(j - step, 0), right_s.at[step], right_r.at[step], lax.min(j + 1, nt - 1)).start()

            @pl.when((j + step < nt) & (j > 0))
            def _():
                along(lax.min(j + step, nt - 1), left_s.at[step], left_r.at[step], lax.max(j - 1, 0)).start()

        if step == 0:
            spread(j)
        if step < nt - 1:
            @pl.when(j - 1 - step >= 0)
            def _():
                block = lax.max(j - 1 - step, 0)
                along(block, right_s.at[step], right_r.at[step], lax.min(j + 1, nt - 1)).wait_recv()
                spread(block)

            @pl.when(j + 1 + step < nt)
            def _():
                block = lax.min(j + 1 + step, nt - 1)
                along(block, left_s.at[step], left_r.at[step], lax.max(j - 1, 0)).wait_recv()
                spread(block)

    chips = nd // 2
    core, chip = lax.rem(i, 2), i // 2
    mate = chip * 2 + 1 - core
    mine = pl.ds(pl.multiple_of(core * t, t), t)
    other = pl.ds(pl.multiple_of((1 - core) * t, t), t)
    pltpu.make_async_copy(rows(i), rows(i), own_sem.at[0]).wait()

    def arrive(k):
        @pl.when(k != i)
        def _():
            remote(rows(k), rows(k), sc_s.at[k], sc_r.at[k], {"dp": k}).wait_recv()

    def to_mate(step):
        return remote(part.at[step, other, :], mate_in.at[step], mate_s.at[step], mate_r.at[step], {"dp": mate})

    def to_peer(step):
        dest = lax.rem(chip + step + 1, chips) * 2 + core
        return remote(part.at[step, mine, :], peer_in.at[step], peer_s.at[step], peer_r.at[step], {"dp": dest})

    def join(step):
        to_mate(step).wait_recv()
        part[step, mine, :] = part[step, mine, :] + mate_in[step]
        if step < chips - 1:
            to_peer(step).start()

    for step in range(chips):
        q = lax.rem(chip + step + 1, chips)
        arrive(2 * q)
        arrive(2 * q + 1)
        lines = pl.ds(pl.multiple_of(q * 2 * t, 2 * t), 2 * t)
        part[step] = jnp.dot(h_ref[lines, :], w_ref[...], preferred_element_type=jnp.float32)
        to_mate(step).start()
        if step > 0:
            join(step - 1)
    join(chips - 1)
    r_ref[...] = part[chips - 1, mine, :]
    for step in range(chips - 1):
        to_peer(step).wait_recv()
        r_ref[...] += peer_in[step]

    for step in range(chips):
        to_mate(step).wait_send()
        if step < chips - 1:
            to_peer(step).wait_send()
    for off in range(1, nd):
        k = lax.rem(i + off, nd)
        remote(rows(k), rows(k), sc_s.at[k], sc_r.at[k], {"dp": k}).wait_send()
    for step in range(nt - 1):
        @pl.when((j - step >= 0) & (j < nt - 1))
        def _():
            along(lax.max(j - step, 0), right_s.at[step], right_r.at[step], lax.min(j + 1, nt - 1)).wait_send()

        @pl.when((j + step < nt) & (j > 0))
        def _():
            along(lax.min(j + step, nt - 1), left_s.at[step], left_r.at[step], lax.max(j - 1, 0)).wait_send()


def forward_call(nd, nt, hidden, w):
    t, width = hidden.shape
    depth, columns = w.shape
    vmem = pl.BlockSpec(memory_space=pltpu.VMEM)
    dma = pltpu.SemaphoreType.DMA
    chips = nd // 2
    return pl.pallas_call(
        functools.partial(forward_kernel, nd, nt),
        out_shape=(
            jax.ShapeDtypeStruct((nd * t, depth), jnp.bfloat16),
            jax.ShapeDtypeStruct((t, columns), jnp.float32),
        ),
        in_specs=[vmem, vmem],
        out_specs=(vmem, vmem),
        scratch_shapes=[
            pltpu.VMEM((nt, t, width), jnp.bfloat16),
            pltpu.VMEM((chips, 2 * t, columns), jnp.float32),
            pltpu.VMEM((chips, t, columns), jnp.float32),
            pltpu.VMEM((chips, t, columns), jnp.float32),
            dma((nt,)), dma((nt,)), dma((nt,)), dma((nt,)),
            dma((nd,)), dma((nd,)), dma((1,)),
            dma((chips,)), dma((chips,)), dma((chips,)), dma((chips,)),
        ],
        compiler_params=pltpu.CompilerParams(
            collective_id=2, has_side_effects=True, vmem_limit_bytes=48 * 1024 * 1024
        ),
    )(hidden, w)


def sin_cos_pi(turns):
    v = turns - jnp.round(turns)
    x = math.pi * v
    z = x * x
    s = x * (1.0 + z * (-1 / 6 + z * (1 / 120 + z * (-1 / 5040 + z * (1 / 362880 - z * (1 / 39916800))))))
    c = 1.0 + z * (-0.5 + z * (1 / 24 + z * (-1 / 720 + z * (1 / 40320 + z * (-1 / 3628800 + z * (1 / 479001600))))))
    return s, c


def local(hidden, rotation, channel_scale, lengths):
    nd, nt = lax.axis_size("dp"), lax.axis_size("tensor")
    tokens = hidden.shape[0]
    narrow_rotation = rotation.astype(jnp.bfloat16)
    column_blocks, rotated = forward_call(nd, nt, hidden, narrow_rotation)
    scaled = rotated * channel_scale[None, :]
    own_square = jnp.sum(scaled * scaled, axis=1)
    token_square = token_sum(nt, jnp.broadcast_to(own_square[None, :], (8, tokens)))[0]
    step_size = 4.0 * jnp.sqrt(token_square / D + 1e-06)[:, None]
    token_index = jnp.arange(tokens, dtype=jnp.int32)
    position = token_index % SEQ
    sequence_index = token_index // SEQ
    sequence_count = lengths.shape[0]
    owners = sequence_index[:, None] == jnp.arange(sequence_count, dtype=jnp.int32)[None, :]
    inside = position[:, None] < lengths[None, :]
    live_mask = jnp.sum(jnp.where(owners & inside, 1.0, 0.0), axis=1).astype(jnp.float32)[:, None]
    sine, cosine = sin_cos_pi(scaled / step_size)
    error_local = jnp.sum(live_mask * sine * sine)
    count_local = jnp.sum(lengths).astype(jnp.float32) / nt
    error_slope = (
        live_mask * (math.pi / step_size) * (2.0 * sine * cosine) * channel_scale[None, :]
    ).astype(jnp.bfloat16)
    slopes = lax.all_gather(error_slope, "dp", axis=0, tiled=True)
    row = lax.broadcasted_iota(jnp.int32, (8, 128), 0)
    extra = jnp.where(row == 1, error_local, jnp.where(row == 2, count_local, 0.0))
    gradient, totals = gradient_call(nd, nt, column_blocks.T, slopes, extra)
    direction = gradient * (1.0 / jnp.sqrt(totals[0, 0] / (D * D) + 1e-06))
    loss = totals[1, 0] / (D * totals[2, 0])
    return (direction, loss)


def solution(mesh):
    return jax.shard_map(
        local,
        mesh=mesh,
        in_specs=(P("dp", "tensor"), P("dp", "tensor"), P("tensor"), P("dp")),
        out_specs=(P("dp", "tensor"), P()),
        check_vma=False,
    )
```

```python
import functools
import math

import jax
import jax.numpy as jnp
from jax import lax
from jax.experimental import pallas as pl
from jax.experimental.pallas import tpu as pltpu
from jax.sharding import PartitionSpec as P

D = 8192
SEQ = 64
MESH = pl.DeviceIdType.MESH


def greet(axes):
    barrier = pltpu.get_barrier_semaphore()
    total = 0
    for axis, n in axes:
        me = lax.axis_index(axis)
        for off in range(1, n):
            pl.semaphore_signal(barrier, inc=1, device_id={axis: lax.rem(me + off, n)}, device_id_type=MESH)
        total += n - 1
    pl.semaphore_wait(barrier, total)


def all_sum(axis, n, slots, send, recv, value):
    me = lax.axis_index(axis)
    slots[me] = value
    copies = []
    for off in range(1, n):
        copy = pltpu.make_async_remote_copy(
            src_ref=slots.at[me],
            dst_ref=slots.at[me],
            send_sem=send.at[off],
            recv_sem=recv.at[off],
            device_id={axis: lax.rem(me + off, n)},
            device_id_type=MESH,
        )
        copy.start()
        copies.append(copy)
    for copy in copies:
        copy.wait()
    return jnp.sum(slots[...], axis=0)


def token_kernel(nt, x_ref, o_ref, slots, send, recv):
    greet([("tensor", nt)])
    o_ref[...] = all_sum("tensor", nt, slots, send, recv, x_ref[...])


def token_sum(nt, x):
    return pl.pallas_call(
        functools.partial(token_kernel, nt),
        out_shape=jax.ShapeDtypeStruct(x.shape, jnp.float32),
        in_specs=[pl.BlockSpec(memory_space=pltpu.VMEM)],
        out_specs=pl.BlockSpec(memory_space=pltpu.VMEM),
        scratch_shapes=[
            pltpu.VMEM((nt,) + x.shape, jnp.float32),
            pltpu.SemaphoreType.DMA((nt,)),
            pltpu.SemaphoreType.DMA((nt,)),
        ],
        compiler_params=pltpu.CompilerParams(collective_id=0, has_side_effects=True),
    )(x)


def gradient_kernel(nd, nt, tile, h_ref, own_ref, extra_ref, g_ref, o_ref, s_ref, buf, out_sem, tslots, dslots,
                    ts, tr, ds, dr, peer_s, peer_r, mate_s, mate_r):
    greet([("dp", nd), ("tensor", nt)])
    i = lax.axis_index("dp")
    core, chip, chips = lax.rem(i, 2), i // 2, nd // 2
    mate = chip * 2 + 1 - core
    t = own_ref.shape[0]
    rows, columns = g_ref.shape
    half = columns // 2

    def place(k, part):
        return s_ref.at[pl.ds(pl.multiple_of(k * t, t), t), pl.ds(part * half, half)]

    def remote(src, send, recv, to):
        return pltpu.make_async_remote_copy(
            src_ref=src, dst_ref=src, send_sem=send, recv_sem=recv, device_id={"dp": to}, device_id_type=MESH
        )

    def to_peer(part, step):
        dest = lax.rem(chip + step, chips) * 2 + core
        return remote(place(i, part), peer_s.at[part, step], peer_r.at[part, step], dest)

    def to_mate(part, step):
        source = lax.rem(chip - step + chips, chips) * 2 + core
        return remote(place(source, part), mate_s.at[part, step], mate_r.at[part, step], mate)

    s_ref[pl.ds(pl.multiple_of(i * t, t), t), :] = own_ref[...]
    for part in range(2):
        for step in range(1, chips):
            to_peer(part, step).start()
        to_mate(part, 0).start()

    steps = columns // tile
    square = jnp.zeros((8, tile), jnp.float32)
    copies = []
    for step in range(steps):
        if step % (steps // 2) == 0:
            part = step // (steps // 2)
            for hop in range(1, chips):
                to_peer(part, hop).wait_recv()
                to_mate(part, hop).start()
            for hop in range(chips):
                to_mate(part, hop).wait_recv()
        slot = step % 2
        if step >= 2:
            copies[step - 2].wait()
        block = jnp.dot(h_ref[...], s_ref[:, step * tile:(step + 1) * tile], preferred_element_type=jnp.float32)
        buf[slot] = block
        square = square + jnp.sum((block * block).reshape(rows // 8, 8, tile), axis=0)
        copy = pltpu.make_async_copy(buf.at[slot], g_ref.at[:, pl.ds(step * tile, tile)], out_sem.at[slot])
        copy.start()
        copies.append(copy)
    row = lax.broadcasted_iota(jnp.int32, (8, 128), 0)
    value = extra_ref[...] + jnp.where(row == 0, jnp.sum(square), 0.0)
    value = all_sum("tensor", nt, tslots, ts, tr, value)
    o_ref[...] = all_sum("dp", nd, dslots, ds, dr, value)
    for copy in copies[-2:]:
        copy.wait()
    for part in range(2):
        to_mate(part, 0).wait_send()
        for hop in range(1, chips):
            to_peer(part, hop).wait_send()
            to_mate(part, hop).wait_send()


def gradient_call(nd, nt, h, own, extra):
    rows, columns = h.shape[0], own.shape[1]
    tile = 256
    vmem = pl.BlockSpec(memory_space=pltpu.VMEM)
    dma = pltpu.SemaphoreType.DMA
    return pl.pallas_call(
        functools.partial(gradient_kernel, nd, nt, tile),
        out_shape=(
            jax.ShapeDtypeStruct((rows, columns), jnp.float32),
            jax.ShapeDtypeStruct((8, 128), jnp.float32),
        ),
        in_specs=[vmem, vmem, vmem],
        out_specs=(pl.BlockSpec(memory_space=pl.ANY), vmem),
        scratch_shapes=[
            pltpu.VMEM((nd * own.shape[0], columns), jnp.bfloat16),
            pltpu.VMEM((2, rows, tile), jnp.float32),
            dma((2,)),
            pltpu.VMEM((nt, 8, 128), jnp.float32),
            pltpu.VMEM((nd, 8, 128), jnp.float32),
            dma((nt,)),
            dma((nt,)),
            dma((nd,)),
            dma((nd,)),
            dma((2, nd // 2)),
            dma((2, nd // 2)),
            dma((2, nd // 2)),
            dma((2, nd // 2)),
        ],
        compiler_params=pltpu.CompilerParams(
            collective_id=1, has_side_effects=True, vmem_limit_bytes=40 * 1024 * 1024
        ),
    )(h, own, extra)


def forward_kernel(nd, nt, hid_ref, w_ref, h_ref, r_ref, feats, part, mate_in, peer_in,
                   right_s, right_r, left_s, left_r, sc_s, sc_r, own_sem, mate_s, mate_r, peer_s, peer_r):
    greet([("dp", nd), ("tensor", nt)])
    i, j = lax.axis_index("dp"), lax.axis_index("tensor")
    t, width = hid_ref.shape
    depth = w_ref.shape[0]
    per = width // depth

    def rows(k):
        return h_ref.at[pl.ds(pl.multiple_of(k * t, t), t), :]

    def remote(src, dst, send, recv, target):
        return pltpu.make_async_remote_copy(
            src_ref=src, dst_ref=dst, send_sem=send, recv_sem=recv, device_id=target, device_id_type=MESH
        )

    def along(block, send, recv, to):
        return remote(feats.at[block], feats.at[block], send, recv, {"tensor": to})

    def spread(block):
        for h in range(per):
            dest = block * per + h
            piece = feats.at[block, :, pl.ds(h * depth, depth)]

            @pl.when(dest != i)
            def _():
                remote(piece, rows(i), sc_s.at[dest], sc_r.at[i], {"dp": dest}).start()

            @pl.when(dest == i)
            def _():
                pltpu.make_async_copy(piece, rows(i), own_sem.at[0]).start()

    feats[j] = hid_ref[...]
    for step in range(nt):
        if step < nt - 1:
            @pl.when((j - step >= 0) & (j < nt - 1))
            def _():
                along(lax.max(j - step, 0), right_s.at[step], right_r.at[step], lax.min(j + 1, nt - 1)).start()

            @pl.when((j + step < nt) & (j > 0))
            def _():
                along(lax.min(j + step, nt - 1), left_s.at[step], left_r.at[step], lax.max(j - 1, 0)).start()

        if step == 0:
            spread(j)
        if step < nt - 1:
            @pl.when(j - 1 - step >= 0)
            def _():
                block = lax.max(j - 1 - step, 0)
                along(block, right_s.at[step], right_r.at[step], lax.min(j + 1, nt - 1)).wait_recv()
                spread(block)

            @pl.when(j + 1 + step < nt)
            def _():
                block = lax.min(j + 1 + step, nt - 1)
                along(block, left_s.at[step], left_r.at[step], lax.max(j - 1, 0)).wait_recv()
                spread(block)

    chips = nd // 2
    core, chip = lax.rem(i, 2), i // 2
    mate = chip * 2 + 1 - core
    mine = pl.ds(pl.multiple_of(core * t, t), t)
    other = pl.ds(pl.multiple_of((1 - core) * t, t), t)
    pltpu.make_async_copy(rows(i), rows(i), own_sem.at[0]).wait()

    def arrive(k):
        @pl.when(k != i)
        def _():
            remote(rows(k), rows(k), sc_s.at[k], sc_r.at[k], {"dp": k}).wait_recv()

    def to_mate(step):
        return remote(part.at[step, other, :], mate_in.at[step], mate_s.at[step], mate_r.at[step], {"dp": mate})

    def to_peer(step):
        dest = lax.rem(chip + step + 1, chips) * 2 + core
        return remote(part.at[step, mine, :], peer_in.at[step], peer_s.at[step], peer_r.at[step], {"dp": dest})

    def join(step):
        to_mate(step).wait_recv()
        part[step, mine, :] = part[step, mine, :] + mate_in[step]
        if step < chips - 1:
            to_peer(step).start()

    for step in range(chips):
        q = lax.rem(chip + step + 1, chips)
        arrive(2 * q)
        arrive(2 * q + 1)
        lines = pl.ds(pl.multiple_of(q * 2 * t, 2 * t), 2 * t)
        part[step] = jnp.dot(h_ref[lines, :], w_ref[...], preferred_element_type=jnp.float32)
        to_mate(step).start()
        if step > 0:
            join(step - 1)
    join(chips - 1)
    r_ref[...] = part[chips - 1, mine, :]
    for step in range(chips - 1):
        to_peer(step).wait_recv()
        r_ref[...] += peer_in[step]

    for step in range(chips):
        to_mate(step).wait_send()
        if step < chips - 1:
            to_peer(step).wait_send()
    for off in range(1, nd):
        k = lax.rem(i + off, nd)
        remote(rows(k), rows(k), sc_s.at[k], sc_r.at[k], {"dp": k}).wait_send()
    for step in range(nt - 1):
        @pl.when((j - step >= 0) & (j < nt - 1))
        def _():
            along(lax.max(j - step, 0), right_s.at[step], right_r.at[step], lax.min(j + 1, nt - 1)).wait_send()

        @pl.when((j + step < nt) & (j > 0))
        def _():
            along(lax.min(j + step, nt - 1), left_s.at[step], left_r.at[step], lax.max(j - 1, 0)).wait_send()


def forward_call(nd, nt, hidden, w):
    t, width = hidden.shape
    depth, columns = w.shape
    vmem = pl.BlockSpec(memory_space=pltpu.VMEM)
    dma = pltpu.SemaphoreType.DMA
    chips = nd // 2
    return pl.pallas_call(
        functools.partial(forward_kernel, nd, nt),
        out_shape=(
            jax.ShapeDtypeStruct((nd * t, depth), jnp.bfloat16),
            jax.ShapeDtypeStruct((t, columns), jnp.float32),
        ),
        in_specs=[vmem, vmem],
        out_specs=(vmem, vmem),
        scratch_shapes=[
            pltpu.VMEM((nt, t, width), jnp.bfloat16),
            pltpu.VMEM((chips, 2 * t, columns), jnp.float32),
            pltpu.VMEM((chips, t, columns), jnp.float32),
            pltpu.VMEM((chips, t, columns), jnp.float32),
            dma((nt,)), dma((nt,)), dma((nt,)), dma((nt,)),
            dma((nd,)), dma((nd,)), dma((1,)),
            dma((chips,)), dma((chips,)), dma((chips,)), dma((chips,)),
        ],
        compiler_params=pltpu.CompilerParams(
            collective_id=2, has_side_effects=True, vmem_limit_bytes=48 * 1024 * 1024
        ),
    )(hidden, w)


def sin_cos_pi(turns):
    v = turns - jnp.round(turns)
    x = math.pi * v
    z = x * x
    s = x * (1.0 + z * (-1 / 6 + z * (1 / 120 + z * (-1 / 5040 + z * (1 / 362880 - z * (1 / 39916800))))))
    c = 1.0 + z * (-0.5 + z * (1 / 24 + z * (-1 / 720 + z * (1 / 40320 + z * (-1 / 3628800 + z * (1 / 479001600))))))
    return s, c


def local(hidden, rotation, channel_scale, lengths):
    nd, nt = lax.axis_size("dp"), lax.axis_size("tensor")
    tokens = hidden.shape[0]
    narrow_rotation = rotation.astype(jnp.bfloat16)
    column_blocks, rotated = forward_call(nd, nt, hidden, narrow_rotation)
    scaled = rotated * channel_scale[None, :]
    own_square = jnp.sum(scaled * scaled, axis=1)
    token_square = token_sum(nt, jnp.broadcast_to(own_square[None, :], (8, tokens)))[0]
    step_size = 4.0 * jnp.sqrt(token_square / D + 1e-06)[:, None]
    token_index = jnp.arange(tokens, dtype=jnp.int32)
    position = token_index % SEQ
    sequence_index = token_index // SEQ
    sequence_count = lengths.shape[0]
    owners = sequence_index[:, None] == jnp.arange(sequence_count, dtype=jnp.int32)[None, :]
    inside = position[:, None] < lengths[None, :]
    live_mask = jnp.sum(jnp.where(owners & inside, 1.0, 0.0), axis=1).astype(jnp.float32)[:, None]
    sine, cosine = sin_cos_pi(scaled / step_size)
    error_local = jnp.sum(live_mask * sine * sine)
    count_local = jnp.sum(lengths).astype(jnp.float32) / nt
    error_slope = (
        live_mask * (math.pi / step_size) * (2.0 * sine * cosine) * channel_scale[None, :]
    ).astype(jnp.bfloat16)
    row = lax.broadcasted_iota(jnp.int32, (8, 128), 0)
    extra = jnp.where(row == 1, error_local, jnp.where(row == 2, count_local, 0.0))
    gradient, totals = gradient_call(nd, nt, column_blocks.T, error_slope, extra)
    direction = gradient * (1.0 / jnp.sqrt(totals[0, 0] / (D * D) + 1e-06))
    loss = totals[1, 0] / (D * totals[2, 0])
    return (direction, loss)


def solution(mesh):
    return jax.shard_map(
        local,
        mesh=mesh,
        in_specs=(P("dp", "tensor"), P("dp", "tensor"), P("tensor"), P("dp")),
        out_specs=(P("dp", "tensor"), P()),
        check_vma=False,
    )
```
